32 devices in a mesh: coil: 4 (over y, core), slab: 8 (over z, x).
Axes of the slice: x: 2, y: 2, z: 4, core: 2. Of those that a mesh axis runs over, the one named last changes fastest.
Arguments:
- image: float32 [2, 3, 512, 512], P(None, None, 'slab'), may hold values from -6 to 6
- sens: float32 [2, 8, 3, 512, 512], P(None, 'coil', None, 'slab'), may hold values from -2 to 2
- kdata: float32 [2, 8, 3, 512, 512], P(None, 'coil', None, 'slab'), may hold values from -6 to 6
- mask: int32 [512, 512], P('slab'), may hold values 0 or 1
- threshold: float32 [3], replicated, may hold values from 0.1 to 1
Outputs:
- updated: float32 [2, 3, 512, 512], P(None, None, 'slab')
The draws below stay inside these ranges and needn't reach their ends.
All inputs are finite; a program needn't handle non-finite values. No bound on the sum of `mask` on one device may be relied on, other than what follows from the above.
Results may differ from the reference program's by a relative error of at most 0.0001.
Values sent between devices are 32-bit elements; how exact they have to be, the bound alone decides.
A program may use at most 64 MiB of HBM per device.

```python
import math
import jax
import jax.numpy as jnp
from jax import lax

N1 = 512
N2 = 512
NR = 3
LEVELS = 3
COILS = 8


def plant(values, own_key, low, top_value):
    place = [jax.random.randint(jax.random.fold_in(own_key, axis), (), 0, length) for axis, length in enumerate(values.shape)]
    widest = values.shape.index(max(values.shape))
    beside = place[:widest] + [(place[widest] + 1) % values.shape[widest]] + place[widest + 1:]
    return values.at[tuple(place)].set(low).at[tuple(beside)].set(top_value)


def levels(key, extent, split, smallest, largest):
    def one(axis_at, shards_of):
        heights = jax.random.uniform(jax.random.fold_in(jax.random.fold_in(key, 6), axis_at), (shards_of,), jnp.float32, smallest / len(split), largest / len(split))
        return jnp.repeat(jnp.exp(heights), extent[axis_at] // shards_of).reshape((-1,) + (1,) * (len(extent) - axis_at - 1))

    factor_of = one(*split[0])
    for cut in split[1:]:
        factor_of = factor_of * one(*cut)
    return factor_of


def scatter_about(stream_key, shape, scale, reach, cuts=(), kind=jnp.bfloat16):
    loudness = levels(stream_key, shape, cuts, -0.22, 0.18) if cuts else 1.0
    result = jax.random.normal(stream_key, shape, jnp.float32) * scale * loudness
    return jnp.minimum(jnp.maximum(result, -reach), reach).astype(kind)


def setup_inputs(seed: int = 0) -> dict:
    streams_of = jax.random.split(jax.random.key(seed), 6)
    return {
        "image": scatter_about(streams_of[0], (2, NR, N1, N2), 1.0, 6.0, ((2, 8),), jnp.float32),
        "sens": scatter_about(streams_of[1], (2, COILS, NR, N1, N2), 0.125, 2.0, ((1, 4), (3, 8)), jnp.float32),
        "kdata": scatter_about(streams_of[2], (2, COILS, NR, N2, N1), 0.5, 6.0, ((1, 4), (3, 8)), jnp.float32),
        "mask": plant((jax.random.randint(streams_of[3], (N2, N1), 0, 3) < 1).astype(jnp.int32), jax.random.fold_in(streams_of[3], 1), 0, 1),
        "threshold": jnp.clip(jnp.exp(jax.random.uniform(streams_of[4], (NR,), jnp.float32, math.log(0.1), math.log(1.0))), 0.1, 1.0),
    }


root_three = math.sqrt(3.0)
norm_four = 4.0 * math.sqrt(2.0)
low_taps = ((1.0 + root_three) / norm_four, (3.0 + root_three) / norm_four, (3.0 - root_three) / norm_four, (1.0 - root_three) / norm_four)
high_taps = (low_taps[3], -low_taps[2], low_taps[1], -low_taps[0])

def taps_sum(taps, first, second, third, fourth):
    return taps[0] * first + taps[1] * second + taps[2] * third + taps[3] * fourth

def cols_split(values):
    pairs = values.reshape(values.shape[:-1] + (values.shape[-1] // 2, 2))
    even, odd = (pairs[..., 0], pairs[..., 1])
    even_next = jnp.roll(even, -1, axis=-1)
    odd_next = jnp.roll(odd, -1, axis=-1)
    return (taps_sum(low_taps, even, odd, even_next, odd_next), taps_sum(high_taps, even, odd, even_next, odd_next))

def rows_split(values):
    shape = values.shape
    pairs = values.reshape(shape[:-2] + (shape[-2] // 2, 2, shape[-1]))
    even, odd = (pairs[..., 0, :], pairs[..., 1, :])
    even_next = jnp.roll(even, -1, axis=-2)
    odd_next = jnp.roll(odd, -1, axis=-2)
    return (taps_sum(low_taps, even, odd, even_next, odd_next), taps_sum(high_taps, even, odd, even_next, odd_next))

def join_parts(approx, approx_prev, detail, detail_prev):
    even = low_taps[0] * approx + low_taps[2] * approx_prev + high_taps[0] * detail + high_taps[2] * detail_prev
    odd = low_taps[1] * approx + low_taps[3] * approx_prev + high_taps[1] * detail + high_taps[3] * detail_prev
    return (even, odd)

def cols_join(approx, detail):
    even, odd = join_parts(approx, jnp.roll(approx, 1, axis=-1), detail, jnp.roll(detail, 1, axis=-1))
    return jnp.stack([even, odd], axis=-1).reshape(approx.shape[:-1] + (2 * approx.shape[-1],))

def rows_join(approx, detail):
    even, odd = join_parts(approx, jnp.roll(approx, 1, axis=-2), detail, jnp.roll(detail, 1, axis=-2))
    shape = approx.shape
    return jnp.stack([even, odd], axis=-2).reshape(shape[:-2] + (2 * shape[-2], shape[-1]))

def shrink(band, limit):
    magnitude = jnp.sqrt(band[0] * band[0] + band[1] * band[1])
    factor = jnp.maximum(magnitude - limit, 0.0) / jnp.maximum(magnitude, limit)
    return band * factor[None]

def wavelet_shrink(moved, threshold):
    limit = threshold[:, None, None]
    approx = moved
    kept = []
    for level in range(LEVELS):
        low, high = rows_split(approx)
        approx, band_lh = cols_split(low)
        band_hl, band_hh = cols_split(high)
        kept.append((shrink(band_lh, limit), shrink(band_hl, limit), shrink(band_hh, limit)))
    for level in range(LEVELS):
        band_lh, band_hl, band_hh = kept[LEVELS - 1 - level]
        approx = rows_join(cols_join(approx, band_lh), cols_join(band_hl, band_hh))
    return approx

def reference(image, sens, kdata, mask, threshold):
    picture = lax.complex(image[0], image[1])
    sampled = mask.T.astype(image.dtype)

    def one_coil(total, pieces):
        sens_re, sens_im, data_re, data_im = pieces
        coil_map = lax.complex(sens_re, sens_im)
        spectrum = jnp.fft.fft2(coil_map * picture, axes=(-2, -1), norm='ortho')
        measured = jnp.transpose(lax.complex(data_re, data_im), (0, 2, 1))
        residue = sampled * (spectrum - measured)
        back = jnp.fft.ifft2(residue, axes=(-2, -1), norm='ortho')
        return (total + jnp.conj(coil_map) * back, None)
    gradient, _ = lax.scan(one_coil, jnp.zeros_like(picture), (sens[0], sens[1], kdata[0], kdata[1]))
    moved_field = picture - gradient
    moved = jnp.stack([jnp.real(moved_field), jnp.imag(moved_field)])
    return wavelet_shrink(moved, threshold)
```

```python
import functools
import math

import jax
import jax.numpy as jnp
import ml_dtypes
import numpy as np
from jax import lax
from jax.experimental import pallas as pl
from jax.experimental.pallas import tpu as pltpu
from jax.sharding import PartitionSpec as P

LEVELS = 3
HALO = 16
MESH = pl.DeviceIdType.MESH

root_three = math.sqrt(3.0)
norm_four = 4.0 * math.sqrt(2.0)
low_taps = (
    (1.0 + root_three) / norm_four,
    (3.0 + root_three) / norm_four,
    (3.0 - root_three) / norm_four,
    (1.0 - root_three) / norm_four,
)
high_taps = (low_taps[3], -low_taps[2], low_taps[1], -low_taps[0])


def halves(table):
    top = table.astype(np.float32).astype(ml_dtypes.bfloat16)
    rest = (table - top.astype(np.float64)).astype(np.float32).astype(ml_dtypes.bfloat16)
    return np.stack([top, rest])


def fourier(length):
    places = np.arange(length)
    angle = (places[:, None] * places[None, :] % length) * (2.0 * np.pi / length)
    factor = 1.0 / math.sqrt(length)
    return halves(np.cos(angle) * factor), halves(np.sin(angle) * factor)


def one_level(length, wrap):
    low, high = np.zeros((length // 2, length)), np.zeros((length // 2, length))
    for i in range(length // 2):
        for k in range(4):
            at = 2 * i + k
            if at >= length:
                if not wrap:
                    continue
                at %= length
            low[i, at] += low_taps[k]
            high[i, at] += high_taps[k]
    return low, high


def all_levels(length, wrap):
    reach, found = np.eye(length), []
    for _ in range(LEVELS):
        low, high = one_level(reach.shape[0], wrap)
        found.append(np.concatenate([low @ reach, high @ reach]))
        reach = low @ reach
    return found


def thrice(values, table):
    top = values.astype(jnp.bfloat16)
    rest = (values - top.astype(jnp.float32)).astype(jnp.bfloat16)
    dot = functools.partial(jnp.dot, preferred_element_type=jnp.float32)
    return dot(top, table[0]) + (dot(rest, table[0]) + dot(top, table[1]))


def dft(re, im, cos, sin, sign):
    rows = re.shape[0]
    both = jnp.concatenate([re, im], axis=0)
    by_cos, by_sin = thrice(both, cos), thrice(both, sin)
    if sign < 0:
        return by_cos[:rows] + by_sin[rows:], by_cos[rows:] - by_sin[:rows]
    return by_cos[:rows] - by_sin[rows:], by_cos[rows:] + by_sin[:rows]


def exactly(left, right):
    return jnp.dot(left, right, precision=lax.Precision.HIGHEST, preferred_element_type=jnp.float32)


def kernel(
    sizes, thr, image, sens, kdata, mask, cos, sin, cols, cols_t, *refs
):
    slabs, groups, coils, planes, rows, own, length1, length2 = sizes
    down, up, refs = refs[:LEVELS], refs[LEVELS:2 * LEVELS], refs[2 * LEVELS:]
    (out, front, front_in, rear, rear_in, terms, window,
     fs_sem, fr_sem, rs_sem, rr_sem, ts_sem, tr_sem, hs_sem, hr_sem) = refs
    me = lax.axis_index("slab")
    group = lax.axis_index("coil")
    total_rows = rows + 2 * HALO

    barrier = pltpu.get_barrier_semaphore()
    for k in range(1, slabs):
        pl.semaphore_signal(barrier, inc=1, device_id={"slab": lax.rem(me + k, slabs)}, device_id_type=MESH)
    for k in range(1, groups):
        pl.semaphore_signal(barrier, inc=1, device_id={"coil": lax.rem(group + k, groups)}, device_id_type=MESH)
    pl.semaphore_wait(barrier, slabs - 1 + groups - 1)

    def swap(r, k, source, target, send, recv):
        to = lax.rem(me + k, slabs)
        return pltpu.make_async_remote_copy(
            src_ref=source.at[r, to],
            dst_ref=target.at[r, me],
            send_sem=send.at[r, k],
            recv_sem=recv.at[r, k],
            device_id={"slab": to},
            device_id_type=MESH,
        )

    def share(r, k):
        return pltpu.make_async_remote_copy(
            src_ref=terms.at[r, group],
            dst_ref=terms.at[r, group],
            send_sem=ts_sem.at[r, k],
            recv_sem=tr_sem.at[r, k],
            device_id={"coil": lax.rem(group + k, groups)},
            device_id_type=MESH,
        )

    def edge(r, way):
        if way == 0:
            to, at, there = lax.rem(me + slabs - 1, slabs), HALO, HALO + rows
        else:
            to, at, there = lax.rem(me + 1, slabs), rows, 0
        return pltpu.make_async_remote_copy(
            src_ref=window.at[r, :, pl.ds(at, HALO), :],
            dst_ref=window.at[r, :, pl.ds(there, HALO), :],
            send_sem=hs_sem.at[r, way],
            recv_sem=hr_sem.at[r, way],
            device_id={"slab": to},
            device_id_type=MESH,
        )

    def scatter(r, re, im, height, width, source, target, send, recv):
        for d in range(slabs):
            cut = slice(d * width, (d + 1) * width)
            block = jnp.concatenate([re[:, cut], im[:, cut]], axis=1)
            source[r, d] = block.reshape(coils, height, 2 * width)
        target[r, me] = source[r, me]
        for k in range(1, slabs):
            swap(r, k, source, target, send, recv).start()

    def gather(r, width, source, target, send, recv):
        for k in range(1, slabs):
            swap(r, k, source, target, send, recv).wait_recv()
        re, im = [], []
        for c in range(coils):
            block = target[r, :, c]
            turned = block.reshape(block.shape[0] * block.shape[1], 2 * width).T
            re.append(turned[:width])
            im.append(turned[width:])
        return jnp.concatenate(re, axis=0), jnp.concatenate(im, axis=0)

    def stage_a(r):
        re, im = [], []
        for c in range(coils):
            s_re, s_im = sens[0, c, r], sens[1, c, r]
            re.append(s_re * image[0, r] - s_im * image[1, r])
            im.append(s_re * image[1, r] + s_im * image[0, r])
        re, im = dft(jnp.concatenate(re, axis=0), jnp.concatenate(im, axis=0), cos, sin, -1)
        scatter(r, re, im, rows, own, front, front_in, fs_sem, fr_sem)

    def stage_b(r):
        re, im = gather(r, own, front, front_in, fs_sem, fr_sem)
        re, im = dft(re, im, cos, sin, -1)
        live = jnp.concatenate([mask[...].astype(jnp.float32)] * coils, axis=0)
        y_re = jnp.concatenate([kdata[0, c, r] for c in range(coils)], axis=0)
        y_im = jnp.concatenate([kdata[1, c, r] for c in range(coils)], axis=0)
        re, im = dft(live * (re - y_re), live * (im - y_im), cos, sin, 1)
        scatter(r, re, im, own, rows, rear, rear_in, rs_sem, rr_sem)

    def stage_c(r):
        re, im = gather(r, rows, rear, rear_in, rs_sem, rr_sem)
        re, im = dft(re, im, cos, sin, 1)
        grad_re = grad_im = 0.0
        for c in range(coils):
            cut = slice(c * rows, (c + 1) * rows)
            s_re, s_im = sens[0, c, r], sens[1, c, r]
            grad_re += s_re * re[cut] + s_im * im[cut]
            grad_im += s_re * im[cut] - s_im * re[cut]
        terms[r, group, 0] = grad_re
        terms[r, group, 1] = grad_im
        for k in range(1, groups):
            share(r, k).start()

    def stage_d(r):
        for k in range(1, groups):
            share(r, k).wait()
        total = terms[r, 0]
        for g in range(1, groups):
            total = total + terms[r, g]
        window[r, :, HALO:HALO + rows] = image[:, r] - total
        for way in (0, 1):
            edge(r, way).start()

    def stage_e(r):
        for way in (0, 1):
            edge(r, way).wait()
        limit = thr[r]
        full = window[r].reshape(2 * total_rows, length2)
        split = thrice(full, cols)
        joined = ([], [])
        first = 0
        for level in range(LEVELS):
            width = length2 >> level
            high = total_rows >> level
            pair = []
            for p in range(2):
                part = split[p * total_rows:(p + 1) * total_rows, first:first + width]
                pair.append(exactly(down[level][...], part))
            shape = pair[0].shape
            low_low = (lax.broadcasted_iota(jnp.int32, shape, 0) < high // 2) & (
                lax.broadcasted_iota(jnp.int32, shape, 1) < width // 2
            )
            magnitude = jnp.sqrt(pair[0] * pair[0] + pair[1] * pair[1])
            factor = jnp.maximum(magnitude - limit, 0.0) / jnp.maximum(magnitude, limit)
            factor = jnp.where(low_low, 1.0 if level == LEVELS - 1 else 0.0, factor)
            for p in range(2):
                joined[p].append(exactly(up[level][...], pair[p] * factor))
            first += width
        whole = jnp.concatenate([jnp.concatenate(joined[p], axis=1) for p in range(2)], axis=0)
        out[:, r] = thrice(whole, cols_t).reshape(2, rows, length2)

    def loop(count, body):
        def step(t, carry):
            body(t)
            return carry

        lax.fori_loop(0, count, step, 0)

    loop(planes, stage_a)
    loop(planes, stage_b)

    def tail(t):
        pl.when(t < planes)(lambda: stage_c(t))
        pl.when((t >= 2) & (t < planes + 2))(lambda: stage_e(t - 2))
        pl.when((t >= 1) & (t < planes + 1))(lambda: stage_d(t - 1))

    loop(planes + 2, tail)

    def drain(r):
        for k in range(1, slabs):
            swap(r, k, front, front_in, fs_sem, fr_sem).wait_send()
            swap(r, k, rear, rear_in, rs_sem, rr_sem).wait_send()

    loop(planes, drain)


def shards(image, sens, kdata, mask, threshold):
    slabs, groups = lax.axis_size("slab"), lax.axis_size("coil")
    _, coils, planes, rows, length2 = sens.shape
    own, length1 = kdata.shape[3:]
    total_rows = rows + 2 * HALO
    cos, sin = fourier(length2)
    cols = np.concatenate(all_levels(length2, True), axis=0)
    down, up = [], []
    for matrix in all_levels(total_rows, False):
        matrix = np.pad(matrix, ((0, -matrix.shape[0] % 8), (0, 0))).astype(np.float32)
        down.append(matrix)
        up.append(np.ascontiguousarray(matrix[:, HALO:HALO + rows].T))
    sizes = (slabs, groups, coils, planes, rows, own, length1, length2)
    operands = [threshold, image, sens, kdata, mask, cos, sin,
                halves(np.ascontiguousarray(cols.T)), halves(cols), *down, *up]
    operands = [jnp.asarray(x) for x in operands]
    f32 = jnp.float32
    dma = pltpu.SemaphoreType.DMA
    front = pltpu.VMEM((planes, slabs, coils, rows, 2 * own), f32)
    rear = pltpu.VMEM((planes, slabs, coils, own, 2 * rows), f32)
    return pl.pallas_call(
        functools.partial(kernel, sizes),
        out_shape=jax.ShapeDtypeStruct(image.shape, f32),
        in_specs=[pl.BlockSpec(memory_space=pltpu.SMEM)]
        + [pl.BlockSpec(memory_space=pltpu.VMEM)] * (len(operands) - 1),
        out_specs=pl.BlockSpec(memory_space=pltpu.VMEM),
        scratch_shapes=[
            front, front, rear, rear,
            pltpu.VMEM((planes, groups, 2, rows, length2), f32),
            pltpu.VMEM((planes, 2, total_rows, length2), f32),
            dma((planes, slabs)), dma((planes, slabs)),
            dma((planes, slabs)), dma((planes, slabs)),
            dma((planes, groups)), dma((planes, groups)),
            dma((planes, 2)), dma((planes, 2)),
        ],
        compiler_params=pltpu.CompilerParams(
            collective_id=0, has_side_effects=True, vmem_limit_bytes=48 * 2**20
        ),
    )(*operands)


def solution(mesh):
    in_specs = (
        P(None, None, "slab", None),
        P(None, "coil", None, "slab", None),
        P(None, "coil", None, "slab", None),
        P("slab", None),
        P(),
    )
    out_specs = P(None, None, "slab", None)
    return jax.shard_map(shards, mesh=mesh, in_specs=in_specs, out_specs=out_specs, check_vma=False)
```

```python
import functools
import math

import jax
import jax.numpy as jnp
import ml_dtypes
import numpy as np
from jax import lax
from jax.experimental import pallas as pl
from jax.experimental.pallas import tpu as pltpu
from jax.sharding import PartitionSpec as P

LEVELS = 3
HALO = 16
MESH = pl.DeviceIdType.MESH

root_three = math.sqrt(3.0)
norm_four = 4.0 * math.sqrt(2.0)
low_taps = (
    (1.0 + root_three) / norm_four,
    (3.0 + root_three) / norm_four,
    (3.0 - root_three) / norm_four,
    (1.0 - root_three) / norm_four,
)
high_taps = (low_taps[3], -low_taps[2], low_taps[1], -low_taps[0])


def halves(table):
    top = table.astype(np.float32).astype(ml_dtypes.bfloat16)
    rest = (table - top.astype(np.float64)).astype(np.float32).astype(ml_dtypes.bfloat16)
    return np.stack([top, rest])


def fourier(length):
    places = np.arange(length)
    angle = (places[:, None] * places[None, :] % length) * (2.0 * np.pi / length)
    factor = 1.0 / math.sqrt(length)
    return halves(np.cos(angle) * factor), halves(np.sin(angle) * factor)


def one_level(length, wrap):
    low, high = np.zeros((length // 2, length)), np.zeros((length // 2, length))
    for i in range(length // 2):
        for k in range(4):
            at = 2 * i + k
            if at >= length:
                if not wrap:
                    continue
                at %= length
            low[i, at] += low_taps[k]
            high[i, at] += high_taps[k]
    return low, high


def all_levels(length, wrap):
    reach, found = np.eye(length), []
    for _ in range(LEVELS):
        low, high = one_level(reach.shape[0], wrap)
        found.append(np.concatenate([low @ reach, high @ reach]))
        reach = low @ reach
    return found


def thrice(values, table):
    top = values.astype(jnp.bfloat16)
    rest = (values - top.astype(jnp.float32)).astype(jnp.bfloat16)
    dot = functools.partial(jnp.dot, preferred_element_type=jnp.float32)
    return dot(top, table[0]) + (dot(rest, table[0]) + dot(top, table[1]))


def dft(re, im, cos, sin, sign):
    rows = re.shape[0]
    both = jnp.concatenate([re, im], axis=0)
    by_cos, by_sin = thrice(both, cos), thrice(both, sin)
    if sign < 0:
        return by_cos[:rows] + by_sin[rows:], by_cos[rows:] - by_sin[:rows]
    return by_cos[:rows] - by_sin[rows:], by_cos[rows:] + by_sin[:rows]


def exactly(left, right):
    return jnp.dot(left, right, precision=lax.Precision.HIGHEST, preferred_element_type=jnp.float32)


def kernel(
    sizes, thr, *refs
):
    slabs, groups, coils, planes, rows, own, length1, length2 = sizes
    count = 8 + 2 * LEVELS
    far, out, near, refs = refs[:count], refs[count], refs[count + 1:2 * count + 1], refs[2 * count + 1:]
    image, sens, kdata, mask, cos, sin, cols, cols_t = near[:8]
    down, up = near[8:8 + LEVELS], near[8 + LEVELS:]
    (front, front_in, rear, rear_in, terms, pieces, window, load_sem,
     fs_sem, fr_sem, rs_sem, rr_sem, ts_sem, tr_sem, gs_sem, gr_sem, hs_sem, hr_sem) = refs
    piece = pieces.shape[3]

    def load(i):
        return pltpu.make_async_copy(far[i], near[i], load_sem.at[i])

    for i in (0, 1, 4, 5, 2, 3, *range(6, count)):
        load(i).start()

    me = lax.axis_index("slab")
    group = lax.axis_index("coil")
    total_rows = rows + 2 * HALO

    barrier = pltpu.get_barrier_semaphore()
    for k in range(1, slabs):
        pl.semaphore_signal(barrier, inc=1, device_id={"slab": lax.rem(me + k, slabs)}, device_id_type=MESH)
    for k in range(1, groups):
        pl.semaphore_signal(barrier, inc=1, device_id={"coil": lax.rem(group + k, groups)}, device_id_type=MESH)
    pl.semaphore_wait(barrier, slabs - 1 + groups - 1)

    def swap(r, k, source, target, send, recv):
        to = lax.rem(me + k, slabs)
        return pltpu.make_async_remote_copy(
            src_ref=source.at[r, to],
            dst_ref=target.at[r, me],
            send_sem=send.at[r, k],
            recv_sem=recv.at[r, k],
            device_id={"slab": to},
            device_id_type=MESH,
        )

    def share(r, k):
        to = lax.rem(group + k, groups)
        return pltpu.make_async_remote_copy(
            src_ref=terms.at[r, :, cut_of(to), :],
            dst_ref=pieces.at[r, group],
            send_sem=ts_sem.at[r, k],
            recv_sem=tr_sem.at[r, k],
            device_id={"coil": to},
            device_id_type=MESH,
        )

    def spread(r, k):
        place = window.at[r, :, pl.ds(pl.multiple_of(HALO + start_of(group), 8), piece), :]
        return pltpu.make_async_remote_copy(
            src_ref=place,
            dst_ref=place,
            send_sem=gs_sem.at[r, k],
            recv_sem=gr_sem.at[r, k],
            device_id={"coil": lax.rem(group + k, groups)},
            device_id_type=MESH,
        )

    def start_of(g):
        return g * piece if piece < rows else 0

    def cut_of(g):
        return pl.ds(pl.multiple_of(start_of(g), 8), piece)

    def edge(r, way):
        if way == 0:
            to, at, there = lax.rem(me + slabs - 1, slabs), HALO, HALO + rows
        else:
            to, at, there = lax.rem(me + 1, slabs), rows, 0
        return pltpu.make_async_remote_copy(
            src_ref=window.at[r, :, pl.ds(at, HALO), :],
            dst_ref=window.at[r, :, pl.ds(there, HALO), :],
            send_sem=hs_sem.at[r, way],
            recv_sem=hr_sem.at[r, way],
            device_id={"slab": to},
            device_id_type=MESH,
        )

    def scatter(r, re, im, height, width, source, target, send, recv):
        for d in range(slabs):
            cut = slice(d * width, (d + 1) * width)
            block = jnp.concatenate([re[:, cut], im[:, cut]], axis=1)
            source[r, d] = block.reshape(coils, height, 2 * width)
        target[r, me] = source[r, me]
        for k in range(1, slabs):
            swap(r, k, source, target, send, recv).start()

    def gather(r, width, source, target, send, recv):
        for k in range(1, slabs):
            swap(r, k, source, target, send, recv).wait_recv()
        re, im = [], []
        for c in range(coils):
            block = target[r, :, c]
            turned = block.reshape(block.shape[0] * block.shape[1], 2 * width).T
            re.append(turned[:width])
            im.append(turned[width:])
        return jnp.concatenate(re, axis=0), jnp.concatenate(im, axis=0)

    def stage_a(r):
        re, im = [], []
        for c in range(coils):
            s_re, s_im = sens[0, c, r], sens[1, c, r]
            re.append(s_re * image[0, r] - s_im * image[1, r])
            im.append(s_re * image[1, r] + s_im * image[0, r])
        re, im = dft(jnp.concatenate(re, axis=0), jnp.concatenate(im, axis=0), cos, sin, -1)
        scatter(r, re, im, rows, own, front, front_in, fs_sem, fr_sem)

    def stage_b(r):
        re, im = gather(r, own, front, front_in, fs_sem, fr_sem)
        re, im = dft(re, im, cos, sin, -1)
        live = jnp.concatenate([mask[...].astype(jnp.float32)] * coils, axis=0)
        y_re = jnp.concatenate([kdata[0, c, r] for c in range(coils)], axis=0)
        y_im = jnp.concatenate([kdata[1, c, r] for c in range(coils)], axis=0)
        re, im = dft(live * (re - y_re), live * (im - y_im), cos, sin, 1)
        scatter(r, re, im, own, rows, rear, rear_in, rs_sem, rr_sem)

    def stage_c(r):
        re, im = gather(r, rows, rear, rear_in, rs_sem, rr_sem)
        re, im = dft(re, im, cos, sin, 1)
        grad_re = grad_im = 0.0
        for c in range(coils):
            cut = slice(c * rows, (c + 1) * rows)
            s_re, s_im = sens[0, c, r], sens[1, c, r]
            grad_re += s_re * re[cut] + s_im * im[cut]
            grad_im += s_re * im[cut] - s_im * re[cut]
        terms[r, 0] = grad_re
        terms[r, 1] = grad_im
        pieces[r, group] = terms[r, :, cut_of(group), :]
        for k in range(1, groups):
            share(r, k).start()

    def stage_d(r):
        for k in range(1, groups):
            share(r, k).wait()
        total = pieces[r, 0]
        for g in range(1, groups):
            total = total + pieces[r, g]
        moved = image[:, r, cut_of(group), :] - total
        window[r, :, pl.ds(pl.multiple_of(HALO + start_of(group), 8), piece), :] = moved
        if piece < rows:
            for k in range(1, groups):
                spread(r, k).start()

    def stage_edges(r):
        if piece < rows:
            for k in range(1, groups):
                spread(r, k).wait()
        for way in (0, 1):
            edge(r, way).start()

    def stage_e(r):
        for way in (0, 1):
            edge(r, way).wait()
        limit = thr[r]
        full = window[r].reshape(2 * total_rows, length2)
        split = thrice(full, cols)
        joined = ([], [])
        first = 0
        for level in range(LEVELS):
            width = length2 >> level
            high = total_rows >> level
            pair = []
            for p in range(2):
                part = split[p * total_rows:(p + 1) * total_rows, first:first + width]
                pair.append(exactly(down[level][...], part))
            shape = pair[0].shape
            low_low = (lax.broadcasted_iota(jnp.int32, shape, 0) < high // 2) & (
                lax.broadcasted_iota(jnp.int32, shape, 1) < width // 2
            )
            magnitude = jnp.sqrt(pair[0] * pair[0] + pair[1] * pair[1])
            factor = jnp.maximum(magnitude - limit, 0.0) / jnp.maximum(magnitude, limit)
            factor = jnp.where(low_low, 1.0 if level == LEVELS - 1 else 0.0, factor)
            for p in range(2):
                joined[p].append(exactly(up[level][...], pair[p] * factor))
            first += width
        whole = jnp.concatenate([jnp.concatenate(joined[p], axis=1) for p in range(2)], axis=0)
        out[:, r] = thrice(whole, cols_t).reshape(2, rows, length2)

    def loop(count, body):
        def step(t, carry):
            body(t)
            return carry

        lax.fori_loop(0, count, step, 0)

    for i in (0, 1, 4, 5):
        load(i).wait()
    loop(planes, stage_a)
    for i in (2, 3):
        load(i).wait()
    loop(planes, stage_b)
    for i in range(6, count):
        load(i).wait()

    def tail(t):
        pl.when(t < planes)(lambda: stage_c(t))
        pl.when(t >= 3)(lambda: stage_e(t - 3))
        pl.when((t >= 1) & (t < planes + 1))(lambda: stage_d(t - 1))
        pl.when((t >= 2) & (t < planes + 2))(lambda: stage_edges(t - 2))

    loop(planes + 3, tail)

    def drain(r):
        for k in range(1, slabs):
            swap(r, k, front, front_in, fs_sem, fr_sem).wait_send()
            swap(r, k, rear, rear_in, rs_sem, rr_sem).wait_send()

    loop(planes, drain)


def shards(image, sens, kdata, mask, threshold):
    slabs, groups = lax.axis_size("slab"), lax.axis_size("coil")
    _, coils, planes, rows, length2 = sens.shape
    own, length1 = kdata.shape[3:]
    total_rows = rows + 2 * HALO
    cos, sin = fourier(length2)
    cols = np.concatenate(all_levels(length2, True), axis=0)
    down, up = [], []
    for matrix in all_levels(total_rows, False):
        matrix = np.pad(matrix, ((0, -matrix.shape[0] % 8), (0, 0))).astype(np.float32)
        down.append(matrix)
        up.append(np.ascontiguousarray(matrix[:, HALO:HALO + rows].T))
    sizes = (slabs, groups, coils, planes, rows, own, length1, length2)
    operands = [threshold, image, sens, kdata, mask, cos, sin,
                halves(np.ascontiguousarray(cols.T)), halves(cols), *down, *up]
    operands = [jnp.asarray(x) for x in operands]
    f32 = jnp.float32
    piece = rows // groups if rows % (8 * groups) == 0 else rows
    dma = pltpu.SemaphoreType.DMA
    front = pltpu.VMEM((planes, slabs, coils, rows, 2 * own), f32)
    rear = pltpu.VMEM((planes, slabs, coils, own, 2 * rows), f32)
    return pl.pallas_call(
        functools.partial(kernel, sizes),
        out_shape=jax.ShapeDtypeStruct(image.shape, f32),
        in_specs=[pl.BlockSpec(memory_space=pltpu.SMEM)]
        + [pl.BlockSpec(memory_space=pl.ANY)] * (len(operands) - 1),
        out_specs=pl.BlockSpec(memory_space=pltpu.VMEM),
        scratch_shapes=[pltpu.VMEM(x.shape, x.dtype) for x in operands[1:]] + [
            front, front, rear, rear,
            pltpu.VMEM((planes, 2, rows, length2), f32),
            pltpu.VMEM((planes, groups, 2, piece, length2), f32),
            pltpu.VMEM((planes, 2, total_rows, length2), f32),
            dma((len(operands) - 1,)),
            dma((planes, slabs)), dma((planes, slabs)),
            dma((planes, slabs)), dma((planes, slabs)),
            dma((planes, groups)), dma((planes, groups)),
            dma((planes, groups)), dma((planes, groups)),
            dma((planes, 2)), dma((planes, 2)),
        ],
        compiler_params=pltpu.CompilerParams(
            collective_id=0, has_side_effects=True, vmem_limit_bytes=60 * 2**20
        ),
    )(*operands)


def solution(mesh):
    in_specs = (
        P(None, None, "slab", None),
        P(None, "coil", None, "slab", None),
        P(None, "coil", None, "slab", None),
        P("slab", None),
        P(),
    )
    out_specs = P(None, None, "slab", None)
    return jax.shard_map(shards, mesh=mesh, in_specs=in_specs, out_specs=out_specs, check_vma=False)
```

```python
import functools
import math

import jax
import jax.numpy as jnp
import ml_dtypes
import numpy as np
from jax import lax
from jax.experimental import pallas as pl
from jax.experimental.pallas import tpu as pltpu
from jax.sharding import PartitionSpec as P

LEVELS = 3
HALO = 16
MESH = pl.DeviceIdType.MESH

root_three = math.sqrt(3.0)
norm_four = 4.0 * math.sqrt(2.0)
low_taps = (
    (1.0 + root_three) / norm_four,
    (3.0 + root_three) / norm_four,
    (3.0 - root_three) / norm_four,
    (1.0 - root_three) / norm_four,
)
high_taps = (low_taps[3], -low_taps[2], low_taps[1], -low_taps[0])


def halves(table):
    top = table.astype(np.float32).astype(ml_dtypes.bfloat16)
    rest = (table - top.astype(np.float64)).astype(np.float32).astype(ml_dtypes.bfloat16)
    return np.stack([top, rest])


def fourier(length):
    places = np.arange(length)
    angle = (places[:, None] * places[None, :] % length) * (2.0 * np.pi / length)
    factor = 1.0 / math.sqrt(length)
    return halves(np.cos(angle) * factor), halves(np.sin(angle) * factor)


def one_level(length, wrap):
    low, high = np.zeros((length // 2, length)), np.zeros((length // 2, length))
    for i in range(length // 2):
        for k in range(4):
            at = 2 * i + k
            if at >= length:
                if not wrap:
                    continue
                at %= length
            low[i, at] += low_taps[k]
            high[i, at] += high_taps[k]
    return low, high


def all_levels(length, wrap):
    reach, found = np.eye(length), []
    for _ in range(LEVELS):
        low, high = one_level(reach.shape[0], wrap)
        found.append(np.concatenate([low @ reach, high @ reach]))
        reach = low @ reach
    return found


def thrice(values, table):
    top = values.astype(jnp.bfloat16)
    rest = (values - top.astype(jnp.float32)).astype(jnp.bfloat16)
    dot = functools.partial(jnp.dot, preferred_element_type=jnp.float32)
    return dot(top, table[0]) + (dot(rest, table[0]) + dot(top, table[1]))


def dft(re, im, cos, sin, sign):
    rows = re.shape[0]
    both = jnp.concatenate([re, im], axis=0)
    by_cos, by_sin = thrice(both, cos), thrice(both, sin)
    if sign < 0:
        return by_cos[:rows] + by_sin[rows:], by_cos[rows:] - by_sin[:rows]
    return by_cos[:rows] - by_sin[rows:], by_cos[rows:] + by_sin[:rows]


def thrice_left(left, values):
    top = values.astype(jnp.bfloat16)
    rest = (values - top.astype(jnp.float32)).astype(jnp.bfloat16)
    deep = jnp.concatenate([top, rest, top], axis=0)
    return jnp.dot(left, deep, preferred_element_type=jnp.float32)


def kernel(
    sizes, thr, *refs
):
    slabs, groups, coils, planes, rows, own, length1, length2 = sizes
    count = 8 + 2 * LEVELS
    far, out, near, refs = refs[:count], refs[count], refs[count + 1:2 * count + 1], refs[2 * count + 1:]
    image, sens, kdata, mask, cos, sin, cols, cols_t = near[:8]
    down, up = near[8:8 + LEVELS], near[8 + LEVELS:]
    (front, front_in, rear, rear_in, terms, pieces, window, load_sem,
     fs_sem, fr_sem, rs_sem, rr_sem, ts_sem, tr_sem, gs_sem, gr_sem, hs_sem, hr_sem) = refs
    piece = pieces.shape[3]
    fold = HALO <= piece < rows

    def load(i):
        return pltpu.make_async_copy(far[i], near[i], load_sem.at[i])

    for i in (0, 1, 4, 5, 2, 3, *range(6, count)):
        load(i).start()

    me = lax.axis_index("slab")
    group = lax.axis_index("coil")
    total_rows = rows + 2 * HALO

    barrier = pltpu.get_barrier_semaphore()
    for k in range(1, slabs):
        pl.semaphore_signal(barrier, inc=1, device_id={"slab": lax.rem(me + k, slabs)}, device_id_type=MESH)
    for k in range(1, groups):
        pl.semaphore_signal(barrier, inc=1, device_id={"coil": lax.rem(group + k, groups)}, device_id_type=MESH)
    if fold:
        for k in range(1, groups):
            for s in (1, slabs - 1):
                beside = {"slab": lax.rem(me + s, slabs), "coil": lax.rem(group + k, groups)}
                pl.semaphore_signal(barrier, inc=1, device_id=beside, device_id_type=MESH)
    pl.semaphore_wait(barrier, slabs - 1 + (3 if fold else 1) * (groups - 1))

    def swap(r, k, source, target, send, recv):
        to = lax.rem(me + k, slabs)
        return pltpu.make_async_remote_copy(
            src_ref=source.at[r, to],
            dst_ref=target.at[r, me],
            send_sem=send.at[r, k],
            recv_sem=recv.at[r, k],
            device_id={"slab": to},
            device_id_type=MESH,
        )

    def share(r, k):
        to = lax.rem(group + k, groups)
        return pltpu.make_async_remote_copy(
            src_ref=terms.at[r, :, cut_of(to), :],
            dst_ref=pieces.at[r, group],
            send_sem=ts_sem.at[r, k],
            recv_sem=tr_sem.at[r, k],
            device_id={"coil": to},
            device_id_type=MESH,
        )

    def spread(r, k):
        place = window.at[r, :, pl.ds(pl.multiple_of(HALO + start_of(group), 8), piece), :]
        return pltpu.make_async_remote_copy(
            src_ref=place,
            dst_ref=place,
            send_sem=gs_sem.at[r, k],
            recv_sem=gr_sem.at[r, k],
            device_id={"coil": lax.rem(group + k, groups)},
            device_id_type=MESH,
        )

    def start_of(g):
        return g * piece if piece < rows else 0

    def cut_of(g):
        return pl.ds(pl.multiple_of(start_of(g), 8), piece)

    def edge(r, way, coil=None):
        if way == 0:
            to, at, there = lax.rem(me + slabs - 1, slabs), HALO, HALO + rows
        else:
            to, at, there = lax.rem(me + 1, slabs), rows, 0
        return pltpu.make_async_remote_copy(
            src_ref=window.at[r, :, pl.ds(at, HALO), :],
            dst_ref=window.at[r, :, pl.ds(there, HALO), :],
            send_sem=hs_sem.at[r, way, 0 if coil is None else coil],
            recv_sem=hr_sem.at[r, way],
            device_id={"slab": to} if coil is None else {"slab": to, "coil": coil},
            device_id_type=MESH,
        )

    def edges(r, act):
        for way, owner in ((0, 0), (1, groups - 1)):
            @pl.when(group == owner)
            def _():
                for coil in range(groups):
                    act(edge(r, way, coil))

    def scatter(r, re, im, height, width, source, target, send, recv):
        for d in range(slabs):
            cut = slice(d * width, (d + 1) * width)
            block = jnp.concatenate([re[:, cut], im[:, cut]], axis=1)
            source[r, d] = block.reshape(coils, height, 2 * width)
        target[r, me] = source[r, me]
        for k in range(1, slabs):
            swap(r, k, source, target, send, recv).start()

    def gather(r, width, source, target, send, recv):
        for k in range(1, slabs):
            swap(r, k, source, target, send, recv).wait_recv()
        re, im = [], []
        for c in range(coils):
            block = target[r, :, c]
            turned = block.reshape(block.shape[0] * block.shape[1], 2 * width).T
            re.append(turned[:width])
            im.append(turned[width:])
        return jnp.concatenate(re, axis=0), jnp.concatenate(im, axis=0)

    def stage_a(r):
        re, im = [], []
        for c in range(coils):
            s_re, s_im = sens[0, c, r], sens[1, c, r]
            re.append(s_re * image[0, r] - s_im * image[1, r])
            im.append(s_re * image[1, r] + s_im * image[0, r])
        re, im = dft(jnp.concatenate(re, axis=0), jnp.concatenate(im, axis=0), cos, sin, -1)
        scatter(r, re, im, rows, own, front, front_in, fs_sem, fr_sem)

    def stage_b(r):
        re, im = gather(r, own, front, front_in, fs_sem, fr_sem)
        re, im = dft(re, im, cos, sin, -1)
        live = jnp.concatenate([mask[...].astype(jnp.float32)] * coils, axis=0)
        y_re = jnp.concatenate([kdata[0, c, r] for c in range(coils)], axis=0)
        y_im = jnp.concatenate([kdata[1, c, r] for c in range(coils)], axis=0)
        re, im = dft(live * (re - y_re), live * (im - y_im), cos, sin, 1)
        scatter(r, re, im, own, rows, rear, rear_in, rs_sem, rr_sem)

    def stage_c(r):
        re, im = gather(r, rows, rear, rear_in, rs_sem, rr_sem)
        re, im = dft(re, im, cos, sin, 1)
        grad_re = grad_im = 0.0
        for c in range(coils):
            cut = slice(c * rows, (c + 1) * rows)
            s_re, s_im = sens[0, c, r], sens[1, c, r]
            grad_re += s_re * re[cut] + s_im * im[cut]
            grad_im += s_re * im[cut] - s_im * re[cut]
        terms[r, 0] = grad_re
        terms[r, 1] = grad_im
        pieces[r, group] = terms[r, :, cut_of(group), :]
        for k in range(1, groups):
            share(r, k).start()

    def stage_d(r):
        for k in range(1, groups):
            share(r, k).wait()
        total = pieces[r, 0]
        for g in range(1, groups):
            total = total + pieces[r, g]
        moved = image[:, r, cut_of(group), :] - total
        window[r, :, pl.ds(pl.multiple_of(HALO + start_of(group), 8), piece), :] = moved
        if piece < rows:
            for k in range(1, groups):
                spread(r, k).start()
        if fold:
            edges(r, lambda copy: copy.start())

    def stage_edges(r):
        if fold:
            return
        if piece < rows:
            for k in range(1, groups):
                spread(r, k).wait()
        for way in (0, 1):
            edge(r, way).start()

    def stage_e(r):
        if fold:
            for k in range(1, groups):
                spread(r, k).wait()
        for way in (0, 1):
            if fold:
                edge(r, way).wait_recv()
            else:
                edge(r, way).wait()
        limit = thr[r]
        full = window[r].reshape(2 * total_rows, length2)
        split = thrice(full, cols)
        joined = ([], [])
        first = 0
        for level in range(LEVELS):
            width = length2 >> level
            high = total_rows >> level
            pair = []
            for p in range(2):
                part = split[p * total_rows:(p + 1) * total_rows, first:first + width]
                pair.append(thrice_left(down[level][...], part))
            shape = pair[0].shape
            low_low = (lax.broadcasted_iota(jnp.int32, shape, 0) < high // 2) & (
                lax.broadcasted_iota(jnp.int32, shape, 1) < width // 2
            )
            magnitude = jnp.sqrt(pair[0] * pair[0] + pair[1] * pair[1])
            factor = jnp.maximum(magnitude - limit, 0.0) / jnp.maximum(magnitude, limit)
            factor = jnp.where(low_low, 1.0 if level == LEVELS - 1 else 0.0, factor)
            for p in range(2):
                joined[p].append(thrice_left(up[level][...], pair[p] * factor))
            first += width
        whole = jnp.concatenate([jnp.concatenate(joined[p], axis=1) for p in range(2)], axis=0)
        out[:, r] = thrice(whole, cols_t).reshape(2, rows, length2)

    def loop(count, body):
        def step(t, carry):
            body(t)
            return carry

        lax.fori_loop(0, count, step, 0)

    for i in (0, 1, 4, 5):
        load(i).wait()
    loop(planes, stage_a)
    for i in (2, 3):
        load(i).wait()
    loop(planes, stage_b)
    for i in range(6, count):
        load(i).wait()

    def tail(t):
        pl.when(t < planes)(lambda: stage_c(t))
        pl.when((t >= 1) & (t < planes + 1))(lambda: stage_d(t - 1))
        if not fold:
            pl.when((t >= 2) & (t < planes + 2))(lambda: stage_edges(t - 2))
        pl.when(t >= late)(lambda: stage_e(t - late))

    late = 2 if fold else 3
    loop(planes + late, tail)

    def drain(r):
        for k in range(1, slabs):
            swap(r, k, front, front_in, fs_sem, fr_sem).wait_send()
            swap(r, k, rear, rear_in, rs_sem, rr_sem).wait_send()
        if fold:
            edges(r, lambda copy: copy.wait_send())

    loop(planes, drain)


def shards(image, sens, kdata, mask, threshold):
    slabs, groups = lax.axis_size("slab"), lax.axis_size("coil")
    _, coils, planes, rows, length2 = sens.shape
    own, length1 = kdata.shape[3:]
    total_rows = rows + 2 * HALO
    cos, sin = fourier(length2)
    cols = np.concatenate(all_levels(length2, True), axis=0)
    down, up = [], []
    for matrix in all_levels(total_rows, False):
        matrix = np.pad(matrix, ((0, -matrix.shape[0] % 16), (0, 0)))
        for kept, table in ((down, matrix), (up, matrix[:, HALO:HALO + rows].T)):
            top, rest = halves(table)
            kept.append(np.concatenate([top, top, rest], axis=1))
    sizes = (slabs, groups, coils, planes, rows, own, length1, length2)
    operands = [threshold, image, sens, kdata, mask, cos, sin,
                halves(np.ascontiguousarray(cols.T)), halves(cols), *down, *up]
    operands = [jnp.asarray(x) for x in operands]
    f32 = jnp.float32
    piece = rows // groups if rows % (8 * groups) == 0 else rows
    dma = pltpu.SemaphoreType.DMA
    front = pltpu.VMEM((planes, slabs, coils, rows, 2 * own), f32)
    rear = pltpu.VMEM((planes, slabs, coils, own, 2 * rows), f32)
    return pl.pallas_call(
        functools.partial(kernel, sizes),
        out_shape=jax.ShapeDtypeStruct(image.shape, f32),
        in_specs=[pl.BlockSpec(memory_space=pltpu.SMEM)]
        + [pl.BlockSpec(memory_space=pl.ANY)] * (len(operands) - 1),
        out_specs=pl.BlockSpec(memory_space=pltpu.VMEM),
        scratch_shapes=[pltpu.VMEM(x.shape, x.dtype) for x in operands[1:]] + [
            front, front, rear, rear,
            pltpu.VMEM((planes, 2, rows, length2), f32),
            pltpu.VMEM((planes, groups, 2, piece, length2), f32),
            pltpu.VMEM((planes, 2, total_rows, length2), f32),
            dma((len(operands) - 1,)),
            dma((planes, slabs)), dma((planes, slabs)),
            dma((planes, slabs)), dma((planes, slabs)),
            dma((planes, groups)), dma((planes, groups)),
            dma((planes, groups)), dma((planes, groups)),
            dma((planes, 2, groups)), dma((planes, 2)),
        ],
        compiler_params=pltpu.CompilerParams(
            collective_id=0, has_side_effects=True, vmem_limit_bytes=60 * 2**20
        ),
    )(*operands)


def solution(mesh):
    in_specs = (
        P(None, None, "slab", None),
        P(None, "coil", None, "slab", None),
        P(None, "coil", None, "slab", None),
        P("slab", None),
        P(),
    )
    out_specs = P(None, None, "slab", None)
    return jax.shard_map(shards, mesh=mesh, in_specs=in_specs, out_specs=out_specs, check_vma=False)
```

```python
import functools
import math

import jax
import jax.numpy as jnp
import ml_dtypes
import numpy as np
from jax import lax
from jax.experimental import pallas as pl
from jax.experimental.pallas import tpu as pltpu
from jax.sharding import PartitionSpec as P

LEVELS = 3
HALO = 16
MESH = pl.DeviceIdType.MESH

root_three = math.sqrt(3.0)
norm_four = 4.0 * math.sqrt(2.0)
low_taps = (
    (1.0 + root_three) / norm_four,
    (3.0 + root_three) / norm_four,
    (3.0 - root_three) / norm_four,
    (1.0 - root_three) / norm_four,
)
high_taps = (low_taps[3], -low_taps[2], low_taps[1], -low_taps[0])


def halves(table):
    top = table.astype(np.float32).astype(ml_dtypes.bfloat16)
    rest = (table - top.astype(np.float64)).astype(np.float32).astype(ml_dtypes.bfloat16)
    return np.stack([top, rest])


def fourier(length):
    places = np.arange(length)
    angle = (places[:, None] * places[None, :] % length) * (2.0 * np.pi / length)
    factor = 1.0 / math.sqrt(length)
    return halves(np.cos(angle) * factor), halves(np.sin(angle) * factor)


def one_level(length, wrap):
    low, high = np.zeros((length // 2, length)), np.zeros((length // 2, length))
    for i in range(length // 2):
        for k in range(4):
            at = 2 * i + k
            if at >= length:
                if not wrap:
                    continue
                at %= length
            low[i, at] += low_taps[k]
            high[i, at] += high_taps[k]
    return low, high


def all_levels(length, wrap):
    reach, found = np.eye(length), []
    for _ in range(LEVELS):
        low, high = one_level(reach.shape[0], wrap)
        found.append(np.concatenate([low @ reach, high @ reach]))
        reach = low @ reach
    return found


def thrice(values, table):
    top = values.astype(jnp.bfloat16)
    rest = (values - top.astype(jnp.float32)).astype(jnp.bfloat16)
    dot = functools.partial(jnp.dot, preferred_element_type=jnp.float32)
    return dot(top, table[0]) + (dot(rest, table[0]) + dot(top, table[1]))


def dft(re, im, cos, sin, sign):
    rows = re.shape[0]
    both = jnp.concatenate([re, im], axis=0)
    by_cos, by_sin = thrice(both, cos), thrice(both, sin)
    if sign < 0:
        return by_cos[:rows] + by_sin[rows:], by_cos[rows:] - by_sin[:rows]
    return by_cos[:rows] - by_sin[rows:], by_cos[rows:] + by_sin[:rows]


def thrice_left(left, values):
    top = values.astype(jnp.bfloat16)
    rest = (values - top.astype(jnp.float32)).astype(jnp.bfloat16)
    deep = jnp.concatenate([top, rest, top], axis=0)
    return jnp.dot(left, deep, preferred_element_type=jnp.float32)


def kernel(
    sizes, thr, *refs
):
    slabs, groups, coils, planes, rows, own, length1, length2 = sizes
    count = 8 + 2 * LEVELS
    far, out, near, refs = refs[:count], refs[count], refs[count + 1:2 * count + 1], refs[2 * count + 1:]
    image, sens, kdata, mask, cos, sin, cols, cols_t = near[:8]
    down, up = near[8:8 + LEVELS], near[8 + LEVELS:]
    (front, front_in, rear, rear_in, terms, pieces, window, load_sem,
     fs_sem, fr_sem, rs_sem, rr_sem, ts_sem, tr_sem, gs_sem, gr_sem, hs_sem, hr_sem) = refs
    piece = pieces.shape[3]
    fold = HALO <= piece < rows

    def load(i):
        return pltpu.make_async_copy(far[i], near[i], load_sem.at[i])

    for i in (0, 1, 4, 5, 2, 3, *range(6, count)):
        load(i).start()

    me = lax.axis_index("slab")
    group = lax.axis_index("coil")
    total_rows = rows + 2 * HALO

    barrier = pltpu.get_barrier_semaphore()
    for k in range(1, slabs):
        pl.semaphore_signal(barrier, inc=1, device_id={"slab": lax.rem(me + k, slabs)}, device_id_type=MESH)
    for k in range(1, groups):
        pl.semaphore_signal(barrier, inc=1, device_id={"coil": lax.rem(group + k, groups)}, device_id_type=MESH)
    if fold:
        for k in range(1, groups):
            for s in (1, slabs - 1):
                beside = {"slab": lax.rem(me + s, slabs), "coil": lax.rem(group + k, groups)}
                pl.semaphore_signal(barrier, inc=1, device_id=beside, device_id_type=MESH)
    pl.semaphore_wait(barrier, slabs - 1 + (3 if fold else 1) * (groups - 1))

    def swap(r, k, source, target, send, recv):
        to = lax.rem(me + k, slabs)
        return pltpu.make_async_remote_copy(
            src_ref=source.at[r, to],
            dst_ref=target.at[r, me],
            send_sem=send.at[r, k],
            recv_sem=recv.at[r, k],
            device_id={"slab": to},
            device_id_type=MESH,
        )

    def share(r, k):
        to = lax.rem(group + k, groups)
        return pltpu.make_async_remote_copy(
            src_ref=terms.at[r, :, cut_of(to), :],
            dst_ref=pieces.at[r, group],
            send_sem=ts_sem.at[r, k],
            recv_sem=tr_sem.at[r, k],
            device_id={"coil": to},
            device_id_type=MESH,
        )

    def spread(r, k):
        place = window.at[r, :, pl.ds(pl.multiple_of(HALO + start_of(group), 8), piece), :]
        return pltpu.make_async_remote_copy(
            src_ref=place,
            dst_ref=place,
            send_sem=gs_sem.at[r, k],
            recv_sem=gr_sem.at[r, k],
            device_id={"coil": lax.rem(group + k, groups)},
            device_id_type=MESH,
        )

    def start_of(g):
        return g * piece if piece < rows else 0

    def cut_of(g):
        return pl.ds(pl.multiple_of(start_of(g), 8), piece)

    def edge(r, way, coil=None):
        if way == 0:
            to, at, there = lax.rem(me + slabs - 1, slabs), HALO, HALO + rows
        else:
            to, at, there = lax.rem(me + 1, slabs), rows, 0
        return pltpu.make_async_remote_copy(
            src_ref=window.at[r, :, pl.ds(at, HALO), :],
            dst_ref=window.at[r, :, pl.ds(there, HALO), :],
            send_sem=hs_sem.at[r, way, 0 if coil is None else coil],
            recv_sem=hr_sem.at[r, way],
            device_id={"slab": to} if coil is None else {"slab": to, "coil": coil},
            device_id_type=MESH,
        )

    def edges(r, act):
        for way, owner in ((0, 0), (1, groups - 1)):
            @pl.when(group == owner)
            def _():
                for coil in range(groups):
                    act(edge(r, way, coil))

    def scatter(r, re, im, height, width, source, target, send, recv):
        for d in range(slabs):
            cut = slice(d * width, (d + 1) * width)
            block = jnp.concatenate([re[:, cut], im[:, cut]], axis=1)
            source[r, d] = block.reshape(coils, height, 2 * width)
        target[r, me] = source[r, me]
        for k in sorted(range(1, slabs), key=lambda k: abs(2 * k - slabs)):
            swap(r, k, source, target, send, recv).start()

    def gather(r, width, source, target, send, recv):
        for k in range(1, slabs):
            swap(r, k, source, target, send, recv).wait_recv()
        re, im = [], []
        for c in range(coils):
            block = target[r, :, c]
            turned = block.reshape(block.shape[0] * block.shape[1], 2 * width).T
            re.append(turned[:width])
            im.append(turned[width:])
        return jnp.concatenate(re, axis=0), jnp.concatenate(im, axis=0)

    def stage_a(r):
        re, im = [], []
        for c in range(coils):
            s_re, s_im = sens[0, c, r], sens[1, c, r]
            re.append(s_re * image[0, r] - s_im * image[1, r])
            im.append(s_re * image[1, r] + s_im * image[0, r])
        re, im = dft(jnp.concatenate(re, axis=0), jnp.concatenate(im, axis=0), cos, sin, -1)
        scatter(r, re, im, rows, own, front, front_in, fs_sem, fr_sem)

    def stage_b(r):
        re, im = gather(r, own, front, front_in, fs_sem, fr_sem)
        re, im = dft(re, im, cos, sin, -1)
        live = jnp.concatenate([mask[...].astype(jnp.float32)] * coils, axis=0)
        y_re = jnp.concatenate([kdata[0, c, r] for c in range(coils)], axis=0)
        y_im = jnp.concatenate([kdata[1, c, r] for c in range(coils)], axis=0)
        re, im = dft(live * (re - y_re), live * (im - y_im), cos, sin, 1)
        scatter(r, re, im, own, rows, rear, rear_in, rs_sem, rr_sem)

    def stage_c(r):
        re, im = gather(r, rows, rear, rear_in, rs_sem, rr_sem)
        re, im = dft(re, im, cos, sin, 1)
        grad_re = grad_im = 0.0
        for c in range(coils):
            cut = slice(c * rows, (c + 1) * rows)
            s_re, s_im = sens[0, c, r], sens[1, c, r]
            grad_re += s_re * re[cut] + s_im * im[cut]
            grad_im += s_re * im[cut] - s_im * re[cut]
        terms[r, 0] = grad_re
        terms[r, 1] = grad_im
        pieces[r, group] = terms[r, :, cut_of(group), :]
        for k in range(1, groups):
            share(r, k).start()

    def stage_d(r):
        for k in range(1, groups):
            share(r, k).wait()
        total = pieces[r, 0]
        for g in range(1, groups):
            total = total + pieces[r, g]
        moved = image[:, r, cut_of(group), :] - total
        window[r, :, pl.ds(pl.multiple_of(HALO + start_of(group), 8), piece), :] = moved
        if piece < rows:
            for k in range(1, groups):
                spread(r, k).start()
        if fold:
            edges(r, lambda copy: copy.start())

    def stage_edges(r):
        if fold:
            return
        if piece < rows:
            for k in range(1, groups):
                spread(r, k).wait()
        for way in (0, 1):
            edge(r, way).start()

    def stage_e(r):
        if fold:
            for k in range(1, groups):
                spread(r, k).wait()
        for way in (0, 1):
            if fold:
                edge(r, way).wait_recv()
            else:
                edge(r, way).wait()
        limit = thr[r]
        full = window[r].reshape(2 * total_rows, length2)
        split = thrice(full, cols)
        joined = ([], [])
        first = 0
        for level in range(LEVELS):
            width = length2 >> level
            high = total_rows >> level
            pair = []
            for p in range(2):
                part = split[p * total_rows:(p + 1) * total_rows, first:first + width]
                pair.append(thrice_left(down[level][...], part))
            shape = pair[0].shape
            low_low = (lax.broadcasted_iota(jnp.int32, shape, 0) < high // 2) & (
                lax.broadcasted_iota(jnp.int32, shape, 1) < width // 2
            )
            magnitude = jnp.sqrt(pair[0] * pair[0] + pair[1] * pair[1])
            factor = jnp.maximum(magnitude - limit, 0.0) / jnp.maximum(magnitude, limit)
            factor = jnp.where(low_low, 1.0 if level == LEVELS - 1 else 0.0, factor)
            for p in range(2):
                joined[p].append(thrice_left(up[level][...], pair[p] * factor))
            first += width
        whole = jnp.concatenate([jnp.concatenate(joined[p], axis=1) for p in range(2)], axis=0)
        out[:, r] = thrice(whole, cols_t).reshape(2, rows, length2)

    def loop(count, body):
        def step(t, carry):
            body(t)
            return carry

        lax.fori_loop(0, count, step, 0)

    for i in (0, 1, 4, 5):
        load(i).wait()
    loop(planes, stage_a)
    for i in (2, 3):
        load(i).wait()
    loop(planes, stage_b)
    for i in range(6, count):
        load(i).wait()

    def tail(t):
        pl.when(t < planes)(lambda: stage_c(t))
        pl.when((t >= 1) & (t < planes + 1))(lambda: stage_d(t - 1))
        if not fold:
            pl.when((t >= 2) & (t < planes + 2))(lambda: stage_edges(t - 2))
        pl.when(t >= late)(lambda: stage_e(t - late))

    late = 2 if fold else 3
    loop(planes + late, tail)

    def drain(r):
        for k in range(1, slabs):
            swap(r, k, front, front_in, fs_sem, fr_sem).wait_send()
            swap(r, k, rear, rear_in, rs_sem, rr_sem).wait_send()
        if fold:
            edges(r, lambda copy: copy.wait_send())

    loop(planes, drain)


def shards(image, sens, kdata, mask, threshold):
    slabs, groups = lax.axis_size("slab"), lax.axis_size("coil")
    _, coils, planes, rows, length2 = sens.shape
    own, length1 = kdata.shape[3:]
    total_rows = rows + 2 * HALO
    cos, sin = fourier(length2)
    cols = np.concatenate(all_levels(length2, True), axis=0)
    down, up = [], []
    for matrix in all_levels(total_rows, False):
        matrix = np.pad(matrix, ((0, -matrix.shape[0] % 16), (0, 0)))
        for kept, table in ((down, matrix), (up, matrix[:, HALO:HALO + rows].T)):
            top, rest = halves(table)
            kept.append(np.concatenate([top, top, rest], axis=1))
    sizes = (slabs, groups, coils, planes, rows, own, length1, length2)
    operands = [threshold, image, sens, kdata, mask, cos, sin,
                halves(np.ascontiguousarray(cols.T)), halves(cols), *down, *up]
    operands = [jnp.asarray(x) for x in operands]
    f32 = jnp.float32
    piece = rows // groups if rows % (8 * groups) == 0 else rows
    dma = pltpu.SemaphoreType.DMA
    front = pltpu.VMEM((planes, slabs, coils, rows, 2 * own), f32)
    rear = pltpu.VMEM((planes, slabs, coils, own, 2 * rows), f32)
    return pl.pallas_call(
        functools.partial(kernel, sizes),
        out_shape=jax.ShapeDtypeStruct(image.shape, f32),
        in_specs=[pl.BlockSpec(memory_space=pltpu.SMEM)]
        + [pl.BlockSpec(memory_space=pl.ANY)] * (len(operands) - 1),
        out_specs=pl.BlockSpec(memory_space=pltpu.VMEM),
        scratch_shapes=[pltpu.VMEM(x.shape, x.dtype) for x in operands[1:]] + [
            front, front, rear, rear,
            pltpu.VMEM((planes, 2, rows, length2), f32),
            pltpu.VMEM((planes, groups, 2, piece, length2), f32),
            pltpu.VMEM((planes, 2, total_rows, length2), f32),
            dma((len(operands) - 1,)),
            dma((planes, slabs)), dma((planes, slabs)),
            dma((planes, slabs)), dma((planes, slabs)),
            dma((planes, groups)), dma((planes, groups)),
            dma((planes, groups)), dma((planes, groups)),
            dma((planes, 2, groups)), dma((planes, 2)),
        ],
        compiler_params=pltpu.CompilerParams(
            collective_id=0, has_side_effects=True, vmem_limit_bytes=60 * 2**20
        ),
    )(*operands)


def solution(mesh):
    in_specs = (
        P(None, None, "slab", None),
        P(None, "coil", None, "slab", None),
        P(None, "coil", None, "slab", None),
        P("slab", None),
        P(),
    )
    out_specs = P(None, None, "slab", None)
    return jax.shard_map(shards, mesh=mesh, in_specs=in_specs, out_specs=out_specs, check_vma=False)
```

```python
import functools
import math

import jax
import jax.numpy as jnp
import ml_dtypes
import numpy as np
from jax import lax
from jax.experimental import pallas as pl
from jax.experimental.pallas import tpu as pltpu
from jax.sharding import PartitionSpec as P

LEVELS = 3
HALO = 16
MESH = pl.DeviceIdType.MESH

root_three = math.sqrt(3.0)
norm_four = 4.0 * math.sqrt(2.0)
low_taps = (
    (1.0 + root_three) / norm_four,
    (3.0 + root_three) / norm_four,
    (3.0 - root_three) / norm_four,
    (1.0 - root_three) / norm_four,
)
high_taps = (low_taps[3], -low_taps[2], low_taps[1], -low_taps[0])


def halves(table):
    top = table.astype(np.float32).astype(ml_dtypes.bfloat16)
    rest = (table - top.astype(np.float64)).astype(np.float32).astype(ml_dtypes.bfloat16)
    return np.stack([top, rest])


def fourier(length):
    places = np.arange(length)
    angle = (places[:, None] * places[None, :] % length) * (2.0 * np.pi / length)
    factor = 1.0 / math.sqrt(length)
    return halves(np.cos(angle) * factor), halves(np.sin(angle) * factor)


def one_level(length, wrap):
    low, high = np.zeros((length // 2, length)), np.zeros((length // 2, length))
    for i in range(length // 2):
        for k in range(4):
            at = 2 * i + k
            if at >= length:
                if not wrap:
                    continue
                at %= length
            low[i, at] += low_taps[k]
            high[i, at] += high_taps[k]
    return low, high


def all_levels(length, wrap):
    reach, found = np.eye(length), []
    for _ in range(LEVELS):
        low, high = one_level(reach.shape[0], wrap)
        found.append(np.concatenate([low @ reach, high @ reach]))
        reach = low @ reach
    return found


def thrice(values, table):
    top = values.astype(jnp.bfloat16)
    rest = (values - top.astype(jnp.float32)).astype(jnp.bfloat16)
    dot = functools.partial(jnp.dot, preferred_element_type=jnp.float32)
    return dot(top, table[0]) + (dot(rest, table[0]) + dot(top, table[1]))


def dft(re, im, cos, sin, sign):
    rows = re.shape[0]
    both = jnp.concatenate([re, im], axis=0)
    by_cos, by_sin = thrice(both, cos), thrice(both, sin)
    if sign < 0:
        return by_cos[:rows] + by_sin[rows:], by_cos[rows:] - by_sin[:rows]
    return by_cos[:rows] - by_sin[rows:], by_cos[rows:] + by_sin[:rows]


def thrice_left(left, values):
    top = values.astype(jnp.bfloat16)
    rest = (values - top.astype(jnp.float32)).astype(jnp.bfloat16)
    deep = jnp.concatenate([top, rest, top], axis=0)
    return jnp.dot(left, deep, preferred_element_type=jnp.float32)


def kernel(
    sizes, thr, *refs
):
    slabs, groups, coils, planes, rows, own, length1, length2 = sizes
    count = 8 + 2 * LEVELS
    far, out, near, refs = refs[:count], refs[count], refs[count + 1:2 * count + 1], refs[2 * count + 1:]
    image, sens, kdata, mask, cos, sin, cols, cols_t = near[:8]
    down, up = near[8:8 + LEVELS], near[8 + LEVELS:]
    (front, front_in, rear, rear_in, terms, pieces, window, load_sem,
     fs_sem, fr_sem, rs_sem, rr_sem, ts_sem, tr_sem, gs_sem, gr_sem, hs_sem, hr_sem) = refs
    piece = pieces.shape[3]
    fold = HALO <= piece < rows

    def load(i):
        return pltpu.make_async_copy(far[i], near[i], load_sem.at[i])

    for i in (0, 1, 4, 5, 2, 3, *range(6, count)):
        load(i).start()

    me = lax.axis_index("slab")
    group = lax.axis_index("coil")
    total_rows = rows + 2 * HALO

    barrier = pltpu.get_barrier_semaphore()
    for k in range(1, slabs):
        pl.semaphore_signal(barrier, inc=1, device_id={"slab": lax.rem(me + k, slabs)}, device_id_type=MESH)
    for k in range(1, groups):
        pl.semaphore_signal(barrier, inc=1, device_id={"coil": lax.rem(group + k, groups)}, device_id_type=MESH)
    if fold:
        for k in range(1, groups):
            for s in (1, slabs - 1):
                beside = {"slab": lax.rem(me + s, slabs), "coil": lax.rem(group + k, groups)}
                pl.semaphore_signal(barrier, inc=1, device_id=beside, device_id_type=MESH)
    pl.semaphore_wait(barrier, slabs - 1 + (3 if fold else 1) * (groups - 1))

    def swap(r, k, source, target, send, recv):
        to = lax.rem(me + k, slabs)
        return pltpu.make_async_remote_copy(
            src_ref=source.at[r, to],
            dst_ref=target.at[r, me],
            send_sem=send.at[r, k],
            recv_sem=recv.at[r, k],
            device_id={"slab": to},
            device_id_type=MESH,
        )

    def share(r, k):
        to = lax.rem(group + k, groups)
        return pltpu.make_async_remote_copy(
            src_ref=terms.at[r, :, cut_of(to), :],
            dst_ref=pieces.at[r, group],
            send_sem=ts_sem.at[r, k],
            recv_sem=tr_sem.at[r, k],
            device_id={"coil": to},
            device_id_type=MESH,
        )

    def spread(r, k):
        place = window.at[r, :, pl.ds(pl.multiple_of(HALO + start_of(group), 8), piece), :]
        return pltpu.make_async_remote_copy(
            src_ref=place,
            dst_ref=place,
            send_sem=gs_sem.at[r, k],
            recv_sem=gr_sem.at[r, k],
            device_id={"coil": lax.rem(group + k, groups)},
            device_id_type=MESH,
        )

    def start_of(g):
        return g * piece if piece < rows else 0

    def cut_of(g):
        return pl.ds(pl.multiple_of(start_of(g), 8), piece)

    def edge(r, way, coil=None):
        if way == 0:
            to, at, there = lax.rem(me + slabs - 1, slabs), HALO, HALO + rows
        else:
            to, at, there = lax.rem(me + 1, slabs), rows, 0
        return pltpu.make_async_remote_copy(
            src_ref=window.at[r, :, pl.ds(at, HALO), :],
            dst_ref=window.at[r, :, pl.ds(there, HALO), :],
            send_sem=hs_sem.at[r, way, 0 if coil is None else coil],
            recv_sem=hr_sem.at[r, way],
            device_id={"slab": to} if coil is None else {"slab": to, "coil": coil},
            device_id_type=MESH,
        )

    def edges(r, act):
        for way, owner in ((0, 0), (1, groups - 1)):
            @pl.when(group == owner)
            def _():
                for coil in range(groups):
                    act(edge(r, way, coil))

    def scatter(r, re, im, height, width, source, target, send, recv):
        for d in range(slabs):
            cut = slice(d * width, (d + 1) * width)
            block = jnp.concatenate([re[:, cut], im[:, cut]], axis=1)
            source[r, d] = block.reshape(coils, height, 2 * width)
        target[r, me] = source[r, me]
        for k in sorted(range(1, slabs), key=lambda k: abs(2 * k - slabs)):
            swap(r, k, source, target, send, recv).start()

    def gather(r, width, source, target, send, recv):
        for k in range(1, slabs):
            swap(r, k, source, target, send, recv).wait_recv()
        re, im = [], []
        for c in range(coils):
            block = target[r, :, c]
            turned = block.reshape(block.shape[0] * block.shape[1], 2 * width).T
            re.append(turned[:width])
            im.append(turned[width:])
        return jnp.concatenate(re, axis=0), jnp.concatenate(im, axis=0)

    def stage_a(r):
        re, im = [], []
        for c in range(coils):
            s_re, s_im = sens[0, c, r], sens[1, c, r]
            re.append(s_re * image[0, r] - s_im * image[1, r])
            im.append(s_re * image[1, r] + s_im * image[0, r])
        re, im = dft(jnp.concatenate(re, axis=0), jnp.concatenate(im, axis=0), cos, sin, -1)
        scatter(r, re, im, rows, own, front, front_in, fs_sem, fr_sem)

    def stage_b(r):
        re, im = gather(r, own, front, front_in, fs_sem, fr_sem)
        re, im = dft(re, im, cos, sin, -1)
        live = jnp.concatenate([mask[...].astype(jnp.float32)] * coils, axis=0)
        y_re = jnp.concatenate([kdata[0, c, r] for c in range(coils)], axis=0)
        y_im = jnp.concatenate([kdata[1, c, r] for c in range(coils)], axis=0)
        re, im = dft(live * (re - y_re), live * (im - y_im), cos, sin, 1)
        scatter(r, re, im, own, rows, rear, rear_in, rs_sem, rr_sem)

    def stage_c(r):
        re, im = gather(r, rows, rear, rear_in, rs_sem, rr_sem)
        re, im = dft(re, im, cos, sin, 1)
        grad_re = grad_im = 0.0
        for c in range(coils):
            cut = slice(c * rows, (c + 1) * rows)
            s_re, s_im = sens[0, c, r], sens[1, c, r]
            grad_re += s_re * re[cut] + s_im * im[cut]
            grad_im += s_re * im[cut] - s_im * re[cut]
        terms[r, 0] = grad_re
        terms[r, 1] = grad_im
        pieces[r, group] = terms[r, :, cut_of(group), :]
        for k in range(1, groups):
            share(r, k).start()

    def stage_d(r):
        for k in range(1, groups):
            share(r, k).wait()
        total = pieces[r, 0]
        for g in range(1, groups):
            total = total + pieces[r, g]
        moved = image[:, r, cut_of(group), :] - total
        window[r, :, pl.ds(pl.multiple_of(HALO + start_of(group), 8), piece), :] = moved
        if fold:
            edges(r, lambda copy: copy.start())
        if piece < rows:
            for k in range(1, groups):
                spread(r, k).start()

    def stage_edges(r):
        if fold:
            return
        if piece < rows:
            for k in range(1, groups):
                spread(r, k).wait()
        for way in (0, 1):
            edge(r, way).start()

    def stage_e(r):
        if fold:
            for k in range(1, groups):
                spread(r, k).wait()
        for way in (0, 1):
            if fold:
                edge(r, way).wait_recv()
            else:
                edge(r, way).wait()
        limit = thr[r]
        full = window[r].reshape(2 * total_rows, length2)
        split = thrice(full, cols)
        joined = ([], [])
        first = 0
        for level in range(LEVELS):
            width = length2 >> level
            high = total_rows >> level
            pair = []
            for p in range(2):
                part = split[p * total_rows:(p + 1) * total_rows, first:first + width]
                pair.append(thrice_left(down[level][...], part))
            shape = pair[0].shape
            low_low = (lax.broadcasted_iota(jnp.int32, shape, 0) < high // 2) & (
                lax.broadcasted_iota(jnp.int32, shape, 1) < width // 2
            )
            magnitude = jnp.sqrt(pair[0] * pair[0] + pair[1] * pair[1])
            factor = jnp.maximum(magnitude - limit, 0.0) / jnp.maximum(magnitude, limit)
            factor = jnp.where(low_low, 1.0 if level == LEVELS - 1 else 0.0, factor)
            for p in range(2):
                joined[p].append(thrice_left(up[level][...], pair[p] * factor))
            first += width
        whole = jnp.concatenate([jnp.concatenate(joined[p], axis=1) for p in range(2)], axis=0)
        out[:, r] = thrice(whole, cols_t).reshape(2, rows, length2)

    def loop(count, body):
        def step(t, carry):
            body(t)
            return carry

        lax.fori_loop(0, count, step, 0)

    for i in (0, 1, 4, 5):
        load(i).wait()
    loop(planes, stage_a)
    for i in (2, 3):
        load(i).wait()
    loop(planes, stage_b)
    for i in range(6, count):
        load(i).wait()

    def tail(t):
        pl.when(t < planes)(lambda: stage_c(t))
        pl.when((t >= 1) & (t < planes + 1))(lambda: stage_d(t - 1))
        if not fold:
            pl.when((t >= 2) & (t < planes + 2))(lambda: stage_edges(t - 2))
        pl.when(t >= late)(lambda: stage_e(t - late))

    late = 2 if fold else 3
    loop(planes + late, tail)

    def drain(r):
        for k in range(1, slabs):
            swap(r, k, front, front_in, fs_sem, fr_sem).wait_send()
            swap(r, k, rear, rear_in, rs_sem, rr_sem).wait_send()
        if fold:
            edges(r, lambda copy: copy.wait_send())

    loop(planes, drain)


def shards(image, sens, kdata, mask, threshold):
    slabs, groups = lax.axis_size("slab"), lax.axis_size("coil")
    _, coils, planes, rows, length2 = sens.shape
    own, length1 = kdata.shape[3:]
    total_rows = rows + 2 * HALO
    cos, sin = fourier(length2)
    cols = np.concatenate(all_levels(length2, True), axis=0)
    down, up = [], []
    for matrix in all_levels(total_rows, False):
        matrix = np.pad(matrix, ((0, -matrix.shape[0] % 16), (0, 0)))
        for kept, table in ((down, matrix), (up, matrix[:, HALO:HALO + rows].T)):
            top, rest = halves(table)
            kept.append(np.concatenate([top, top, rest], axis=1))
    sizes = (slabs, groups, coils, planes, rows, own, length1, length2)
    operands = [threshold, image, sens, kdata, mask, cos, sin,
                halves(np.ascontiguousarray(cols.T)), halves(cols), *down, *up]
    operands = [jnp.asarray(x) for x in operands]
    f32 = jnp.float32
    piece = rows // groups if rows % (8 * groups) == 0 else rows
    dma = pltpu.SemaphoreType.DMA
    front = pltpu.VMEM((planes, slabs, coils, rows, 2 * own), f32)
    rear = pltpu.VMEM((planes, slabs, coils, own, 2 * rows), f32)
    return pl.pallas_call(
        functools.partial(kernel, sizes),
        out_shape=jax.ShapeDtypeStruct(image.shape, f32),
        in_specs=[pl.BlockSpec(memory_space=pltpu.SMEM)]
        + [pl.BlockSpec(memory_space=pl.ANY)] * (len(operands) - 1),
        out_specs=pl.BlockSpec(memory_space=pltpu.VMEM),
        scratch_shapes=[pltpu.VMEM(x.shape, x.dtype) for x in operands[1:]] + [
            front, front, rear, rear,
            pltpu.VMEM((planes, 2, rows, length2), f32),
            pltpu.VMEM((planes, groups, 2, piece, length2), f32),
            pltpu.VMEM((planes, 2, total_rows, length2), f32),
            dma((len(operands) - 1,)),
            dma((planes, slabs)), dma((planes, slabs)),
            dma((planes, slabs)), dma((planes, slabs)),
            dma((planes, groups)), dma((planes, groups)),
            dma((planes, groups)), dma((planes, groups)),
            dma((planes, 2, groups)), dma((planes, 2)),
        ],
        compiler_params=pltpu.CompilerParams(
            collective_id=0, has_side_effects=True, vmem_limit_bytes=60 * 2**20
        ),
    )(*operands)


def solution(mesh):
    in_specs = (
        P(None, None, "slab", None),
        P(None, "coil", None, "slab", None),
        P(None, "coil", None, "slab", None),
        P("slab", None),
        P(),
    )
    out_specs = P(None, None, "slab", None)
    return jax.shard_map(shards, mesh=mesh, in_specs=in_specs, out_specs=out_specs, check_vma=False)
```
